32 devices in a mesh: groups: 2 (over y), tensor: 4 (over z), batch: 4 (over x, core).
Axes of the slice: x: 2, y: 2, z: 4, core: 2. Of those that a mesh axis runs over, the one named last changes fastest.
Arguments:
- stream: bfloat16 [1024, 12288], P(('groups', 'batch'), 'tensor'), parts along dimension 0, may hold values from -6 to 6
- ln_gain: bfloat16 [12288], replicated, may hold values from 0.099609375 to 1.8984375
- ln_bias: bfloat16 [12288], replicated, may hold values from -3 to 3
- fc1_weight: bfloat16 [12288, 24576], P('batch', 'tensor'), may hold values from -0.0546875 to 0.0546875
- fc1_bias: bfloat16 [24576], P('tensor'), may hold values from -3 to 3
- fc2_weight: bfloat16 [24576, 12288], P('tensor', 'batch'), may hold values from -0.25 to 0.25
- fc2_bias: bfloat16 [12288], P('tensor'), may hold values from -3 to 3
- active_ids: int32 [8, 16], P('groups'), parts along dimension 0, may hold values from 0 to 191, as said below
- active_counts: int32 [8], P('groups'), parts along dimension 0, may hold values from 4 to 16
Outputs:
- mixed: bfloat16 [1024, 12288], P(('groups', 'batch'), 'tensor'), parts along dimension 0
The draws below stay inside these ranges and needn't reach their ends.
There are 2 independent parts, one for each index of `groups`. The reference program is written for one: setup_inputs(seed, part) draws one part's arguments, and reference() takes and returns one part's arrays. A program takes and returns all parts, laid end to end along the dimension named above; an argument that names none is the same for every part. Nothing has to cross between parts.
Inputs may be any that keep to these rules, and one draw needn't show every extreme that they name: `active_ids`: the first active_counts[r] entries of row r are distinct block numbers; among them at most 4 lie in any range of 48 consecutive blocks starting at a multiple of it, and in every row batch some such range holds exactly 4. Entries after the count are arbitrary block numbers.
All inputs are finite; a program needn't handle non-finite values.
Results may differ from the reference program's by a relative error of at most 0.0051.
Values may be sent and summed in bfloat16 or wider, within the bound.
No kernel may reach another device: no remote copies, remote signals or barrier semaphores. Data moves between devices by JAX's collectives and lax.ppermute only.
A program may use at most 320 MiB of HBM per device.

```python
import jax
import jax.numpy as jnp
from jax import lax

D = 12288
FF = 24576
BLOCK = 128
CAP = 4
ROWS_DEV = 128
ROW_BATCHES = 4
ROWS = 512
BLOCKS = 192
LIST_ENTRIES = 16


def build_block_lists(key):
    tensor_devs = LIST_ENTRIES // CAP
    per_device = BLOCKS // tensor_devs
    key_count, key_pick, key_order, key_fill, key_force = jax.random.split(key, 5)
    key_full = jax.random.fold_in(key_force, 7)
    device_count = jax.random.randint(key_count, (ROW_BATCHES, tensor_devs), 0, CAP + 1)
    offset = jax.random.randint(key_force, (), 0, tensor_devs)
    forced = (jnp.arange(ROW_BATCHES) * 3 + offset) % tensor_devs
    full_row = jax.random.randint(key_full, (), 0, ROW_BATCHES)
    least_row = (full_row + 1) % ROW_BATCHES
    row_index = jnp.arange(ROW_BATCHES)[:, None]
    is_forced = jnp.arange(tensor_devs)[None, :] == forced[:, None]
    device_count = jnp.where(row_index == least_row, 0, device_count)
    device_count = jnp.where(is_forced, CAP, device_count)
    device_count = jnp.where(row_index == full_row, CAP, device_count)
    scores = jax.random.randint(key_pick, (ROW_BATCHES, tensor_devs, per_device), 0, 4096) * per_device + jnp.arange(per_device)
    picked = jnp.argsort(scores, axis=-1, stable=True)[:, :, :CAP]
    chosen = picked + (jnp.arange(tensor_devs) * per_device)[None, :, None]
    valid_flag = (jnp.arange(CAP)[None, None, :] < device_count[:, :, None]).astype(jnp.int32)
    chosen = chosen.reshape(ROW_BATCHES, LIST_ENTRIES)
    valid_flag = valid_flag.reshape(ROW_BATCHES, LIST_ENTRIES)
    rank_key = jax.random.randint(key_order, (ROW_BATCHES, LIST_ENTRIES), 0, 4096) * LIST_ENTRIES + jnp.arange(LIST_ENTRIES)
    sort_key = (1 - valid_flag) * (4096 * LIST_ENTRIES) + rank_key
    sort_order = jnp.argsort(sort_key, axis=-1, stable=True)
    block_ids = jnp.take_along_axis(chosen, sort_order, axis=-1)
    alive_flag = jnp.take_along_axis(valid_flag, sort_order, axis=-1)
    filler = jax.random.randint(key_fill, (ROW_BATCHES, LIST_ENTRIES), 0, BLOCKS)
    listed = jnp.where(alive_flag == 1, block_ids, filler).astype(jnp.int32)
    return (listed, jnp.sum(valid_flag, axis=1).astype(jnp.int32))


def draw_active_ids(key, part):
    return build_block_lists(key)[0]


def draw_active_counts(key, part):
    return build_block_lists(key)[1]


def block_scale(stream_key, dims, cuts, least, high):
    def one(dim, parts):
        draws = jax.random.uniform(jax.random.fold_in(jax.random.fold_in(stream_key, 6), dim), (parts,), jnp.float32, least / len(cuts), high / len(cuts))
        return jnp.repeat(jnp.exp(draws), dims[dim] // parts).reshape((-1,) + (1,) * (len(dims) - dim - 1))

    level = one(*cuts[0])
    for cut in cuts[1:]:
        level = level * one(*cut)
    return level


def centred(own_key, shape, deviation, reach, pieces=(), kind=jnp.bfloat16):
    factor_of = block_scale(own_key, shape, pieces, -0.22, 0.18) if pieces else 1.0
    array = jax.random.normal(own_key, shape, jnp.float32) * deviation * factor_of
    return jnp.minimum(jnp.maximum(array, -reach), reach).astype(kind)


def setup_inputs(seed: int = 0, part: int = 0) -> dict:
    splits = jax.random.split(jax.random.key(seed), 10)
    part_splits = jax.random.split(jax.random.fold_in(splits[9], part), 10)
    return {
        "stream": centred(part_splits[0], (ROWS, D), 1.0, 6.0, ((0, 4), (1, 4))),
        "ln_gain": jnp.clip(1.0 + 0.18 * jax.random.normal(splits[1], (D,), jnp.float32), 0.099609375, 1.8984375).astype(jnp.bfloat16),
        "ln_bias": centred(splits[2], (D,), 0.5, 3.0),
        "fc1_weight": centred(splits[3], (D, FF), D ** -0.5, 0.0546875, ((0, 4), (1, 4))),
        "fc1_bias": centred(splits[4], (FF,), 0.5, 3.0, ((0, 4),)),
        "fc2_weight": centred(splits[5], (FF, D), (LIST_ENTRIES * BLOCK // 4) ** -0.5, 0.25, ((0, 4), (1, 4))),
        "fc2_bias": centred(splits[6], (D,), 0.5, 3.0, ((0, 4),)),
        "active_ids": draw_active_ids(jax.random.fold_in(jax.random.fold_in(splits[9], part), 71), part),
        "active_counts": draw_active_counts(jax.random.fold_in(jax.random.fold_in(splits[9], part), 71), part),
    }


def normalize(values_in, gain, shift):
    values = values_in.astype(jnp.float32)
    center = lax.optimization_barrier(jnp.mean(values, axis=-1, keepdims=True))
    spread = lax.optimization_barrier(jnp.mean(jnp.square(values - center), axis=-1, keepdims=True))
    scaled = (values - center) * lax.rsqrt(spread + 1e-05)
    return (scaled * gain.astype(jnp.float32) + shift.astype(jnp.float32)).astype(jnp.bfloat16)

def reference(stream, ln_gain, ln_bias, fc1_weight, fc1_bias, fc2_weight, fc2_bias, active_ids, active_counts):
    normed = normalize(stream, ln_gain, ln_bias).reshape(ROW_BATCHES, ROWS_DEV, D)
    residual = stream.reshape(ROW_BATCHES, ROWS_DEV, D)
    up_blocks = fc1_weight.reshape(D, BLOCKS, BLOCK)
    up_bias = fc1_bias.reshape(BLOCKS, BLOCK).astype(jnp.float32)
    down_blocks = fc2_weight.reshape(BLOCKS, BLOCK, D)

    def one_batch(packed):
        normed_rows, start_rows, block_ids, block_total = packed
        block_alive_mask = (jnp.arange(LIST_ENTRIES) < block_total).astype(jnp.float32)
        up_taken = jnp.take(up_blocks, block_ids, axis=1).reshape(D, LIST_ENTRIES * BLOCK)
        pre_activation = jnp.dot(normed_rows, up_taken, preferred_element_type=jnp.float32).reshape(ROWS_DEV, LIST_ENTRIES, BLOCK)
        pre_activation = pre_activation + jnp.take(up_bias, block_ids, axis=0)[None]
        hidden_state = (jnp.maximum(pre_activation, 0.0) * block_alive_mask[None, :, None]).astype(jnp.bfloat16)
        down_taken = jnp.take(down_blocks, block_ids, axis=0).reshape(LIST_ENTRIES * BLOCK, D)
        product = jnp.dot(hidden_state.reshape(ROWS_DEV, LIST_ENTRIES * BLOCK), down_taken, preferred_element_type=jnp.float32)
        result = start_rows.astype(jnp.float32) + product + fc2_bias.astype(jnp.float32)
        return result.astype(jnp.bfloat16)
    output_rows = lax.map(one_batch, (normed, residual, active_ids, active_counts))
    return output_rows.reshape(ROWS, D)
```

```python
import functools

import jax
import jax.numpy as jnp
from jax import lax
from jax.experimental import pallas as pl
from jax.experimental.pallas import tpu as pltpu
from jax.sharding import PartitionSpec as P

BLOCK = 128
CAP = 4
PIECES = 2
VMEM_LIMIT = 40 * 1024 * 1024
bf16 = jnp.bfloat16
f32 = jnp.float32

VMEM = pl.BlockSpec(memory_space=pltpu.VMEM)
SMEM = pl.BlockSpec(memory_space=pltpu.SMEM)
ANY = pl.BlockSpec(memory_space=pl.ANY)


def call(body, outs, in_specs, out_specs=None, scratch=(), flops=0, moved=0, aliases=None, grid=()):
    return pl.pallas_call(
        body,
        grid=grid,
        out_shape=outs,
        in_specs=in_specs,
        out_specs=out_specs if out_specs is not None else jax.tree.map(lambda _: VMEM, outs),
        scratch_shapes=list(scratch),
        input_output_aliases=aliases or {},
        compiler_params=pltpu.CompilerParams(vmem_limit_bytes=VMEM_LIMIT),
        cost_estimate=pl.CostEstimate(flops=flops, bytes_accessed=moved, transcendentals=0),
    )


def slots(active_ids, active_counts, local_blocks, tensor_index):
    slot_total = active_ids.shape[1]
    local_ids = active_ids - tensor_index * local_blocks
    present = (
        (jnp.arange(slot_total)[None, :] < active_counts[:, None])
        & (local_ids >= 0)
        & (local_ids < local_blocks)
    )
    present_int = present.astype(jnp.int32)
    position = jnp.cumsum(present_int, axis=1) - 1
    matches = present_int[:, :, None] * (
        position[:, :, None] == jnp.arange(CAP)[None, None, :]
    ).astype(jnp.int32)
    slot_block = jnp.sum(matches * local_ids[:, :, None], axis=1)
    live_total = jnp.sum(present_int, axis=1)
    return slot_block, live_total


def norm_kernel(where_ref, own, near, far, mid, fwd, gain, shift, *rest):
    outs, scr = rest[:4], rest[4]
    rows, width = own.shape
    step = 16
    t, s = where_ref[0], where_ref[1]
    full = 4 * width

    def chunk(i, _):
        at = pl.ds(pl.multiple_of(i * step, step), step)

        def part(k):
            if k == 0:
                return own[at, :].astype(f32)
            if k == 1:
                return near[at, :].astype(f32)
            if k == 2:
                return far[at, :].astype(f32)
            return mid[at, :].astype(f32) + fwd[at, :].astype(f32)

        total = sum(jnp.sum(part(k), axis=1, keepdims=True) for k in range(4))
        center = total / full
        square = sum(
            jnp.sum(jnp.square(part(k) - center), axis=1, keepdims=True) for k in range(4)
        )
        factor = lax.rsqrt(square / full + 1e-05)
        for k in range(4):
            f = jnp.bitwise_xor(t, k)
            scaled = (part(k) - center) * factor
            scr[jnp.bitwise_xor(s, k), at, :] = (scaled * gain[f] + shift[f]).astype(bf16)
        return 0

    lax.fori_loop(0, rows // step, chunk, 0)
    for j in range(4):
        outs[j][...] = scr[j]


def normalize(where, own, near, far, mid, fwd, gain, shift):
    shape = own.shape
    out = jax.ShapeDtypeStruct(shape, bf16)
    return call(
        norm_kernel,
        [out] * 4,
        [SMEM] + [VMEM] * 7,
        scratch=[pltpu.VMEM((4,) + shape, bf16)],
        flops=4 * shape[0] * shape[1] * 12,
        moved=shape[0] * shape[1] * 2 * 9,
    )(where, own, near, far, mid, fwd, gain, shift)


def up_kernel(parts, sid, live, *refs):
    n = len(parts)
    xs, w, outs, buf, sems = refs[:n], refs[n], refs[n + 1 : 2 * n + 1], refs[2 * n + 1], refs[2 * n + 2]

    def copies(q):
        j = parts[q]
        for k in range(CAP):
            at = pl.ds(pl.multiple_of(sid[j, k] * BLOCK, BLOCK), BLOCK)
            yield k < live[j], pltpu.make_async_copy(
                w.at[:, at], buf.at[q, :, pl.ds(k * BLOCK, BLOCK)], sems.at[q, k]
            )

    for q in range(n):
        for on, copy in copies(q):
            pl.when(on)(copy.start)
    for q in range(n):
        for on, copy in copies(q):
            pl.when(on)(copy.wait)
        outs[q][...] = jnp.dot(xs[q][...], buf[q], preferred_element_type=f32).astype(outs[q].dtype)


def up(parts, kinds, sid, live, xs, w):
    n = len(parts)
    rows, width = xs[0].shape
    return call(
        functools.partial(up_kernel, parts),
        [jax.ShapeDtypeStruct((rows, CAP * BLOCK), kind) for kind in kinds],
        [SMEM, SMEM] + [VMEM] * n + [ANY],
        scratch=[pltpu.VMEM((n, width, CAP * BLOCK), bf16), pltpu.SemaphoreType.DMA((n, CAP))],
        flops=n * rows * width * CAP * BLOCK * 2,
        moved=n * width * CAP * BLOCK * 2,
    )(sid, live, *xs, w)


def down_kernel(parts, sid, live, *refs):
    n = len(parts)
    hs, w, outs, buf, sems = refs[:n], refs[n], refs[n + 1 : 2 * n + 1], refs[2 * n + 1], refs[2 * n + 2]

    def copies(q):
        j = parts[q]
        for k in range(CAP):
            at = pl.ds(pl.multiple_of(sid[j, k] * BLOCK, BLOCK), BLOCK)
            yield k < live[j], pltpu.make_async_copy(
                w.at[at, :], buf.at[q, pl.ds(k * BLOCK, BLOCK), :], sems.at[q, k]
            )

    for q in range(n):
        for k, (on, copy) in enumerate(copies(q)):
            pl.when(on)(copy.start)

            @pl.when(jnp.logical_not(on))
            def _():
                buf[q, pl.ds(k * BLOCK, BLOCK), :] = jnp.zeros((BLOCK, buf.shape[2]), bf16)

    for q in range(n):
        for on, copy in copies(q):
            pl.when(on)(copy.wait)
        outs[q][...] = jnp.dot(hs[q][...], buf[q], preferred_element_type=f32).astype(outs[q].dtype)


def down(parts, sid, live, hs, w):
    n = len(parts)
    rows = hs[0].shape[0]
    width = w.shape[1]
    return call(
        functools.partial(down_kernel, parts),
        [jax.ShapeDtypeStruct((rows, width), bf16)] * n,
        [SMEM, SMEM] + [VMEM] * n + [ANY],
        scratch=[pltpu.VMEM((n, CAP * BLOCK, width), bf16), pltpu.SemaphoreType.DMA((n, CAP))],
        flops=n * rows * width * CAP * BLOCK * 2,
        moved=n * width * CAP * BLOCK * 2,
    )(sid, live, *hs, w)


def pair_kernel(p0, p2, r1, r3, s_ref, send):
    rows = p0.shape[0]
    for i, (p, r) in enumerate(((p0, r1), (p2, r3))):
        total = p[...] + r[...].astype(f32)
        at = pl.ds(i * rows, rows)
        s_ref[at, :] = total
        send[at, :] = total.astype(bf16)


def hidden_kernel(live, s_ref, got, bias, out):
    rows = s_ref.shape[0] // 2
    lane = lax.broadcasted_iota(jnp.int32, (rows, CAP * BLOCK), 1)
    for i in range(2):
        at, other = pl.ds(i * rows, rows), pl.ds((1 - i) * rows, rows)
        value = s_ref[at, :] + got[other, :].astype(f32) + bias[i]
        on = lane < live[2 * i] * BLOCK
        out[at, :] = jnp.where(on, jnp.maximum(value, 0.0), 0.0).astype(bf16)


def route_kernel(where_ref, y0, y1, y2, y3, z0, z1, z2, z3, scr):
    s = where_ref[1]
    for j, y in enumerate((y0, y1, y2, y3)):
        scr[jnp.bitwise_xor(s, j)] = y[...]
    for k, z in enumerate((z0, z1, z2, z3)):
        z[...] = scr[k]


def final_kernel(x, z0, k1, mid, k2, bias, *refs):
    out = refs[-1]
    total = x[...].astype(f32) + z0[...].astype(f32) + k1[...].astype(f32)
    total = total + (mid[...].astype(f32) + k2[...].astype(f32)) + bias[...]
    out[...] = total.astype(bf16)


def swap(x, axis, pairs):
    return lax.ppermute(x, axis, pairs)


NEAR = [(0, 1), (1, 0), (2, 3), (3, 2)]
FAR = [(0, 2), (2, 0), (1, 3), (3, 1)]
CROSS = [(0, 3), (3, 0), (1, 2), (2, 1)]
MIDDLE = [(1, 2), (2, 1)]
OUTWARD = [(1, 0), (2, 3)]
INWARD = [(0, 1), (3, 2)]
BATCH = {1: NEAR, 2: FAR, 3: CROSS}


def small_mesh(
    stream, ln_gain, ln_bias, fc1_weight, fc1_bias, fc2_weight, fc2_bias, active_ids, active_counts
):
    t = lax.axis_index("tensor")
    b = lax.axis_index("batch")
    rows, width = stream.shape
    local_blocks = fc1_weight.shape[1] // BLOCK
    m = rows // PIECES

    slot_block, live_total = slots(active_ids, active_counts, local_blocks, t)
    order = jnp.bitwise_xor(b, jnp.arange(4))
    sid = jnp.take(slot_block, order, axis=0)
    live = jnp.take(live_total, order, axis=0)
    bias_table = fc1_bias.reshape(local_blocks, BLOCK).astype(f32)
    up_bias = jnp.take(bias_table, sid[::2], axis=0).reshape(2, 1, CAP * BLOCK)
    where = jnp.stack([t, jnp.bitwise_xor(t, b)]).astype(jnp.int32)
    gain = ln_gain.astype(f32).reshape(4, 1, width)
    shift = ln_bias.astype(f32).reshape(4, 1, width)
    down_bias = fc2_bias.astype(f32).reshape(1, width)

    out = None
    for p in range(PIECES):
        x = stream[p * m : (p + 1) * m]
        far = swap(x, "tensor", FAR)
        near = swap(x, "tensor", NEAR)
        mid = swap(x, "tensor", MIDDLE)
        fwd = swap(far, "tensor", OUTWARD)
        n = normalize(where, x, near, far, mid, fwd, gain, shift)
        n = [n[0]] + [swap(n[j], "batch", BATCH[j]) for j in (1, 2, 3)]
        p0, p1 = up((0, 1), (f32, bf16), sid, live, n[:2], fc1_weight)
        p2, p3 = up((2, 3), (f32, bf16), sid, live, n[2:], fc1_weight)
        r1 = swap(p1, "batch", NEAR)
        r3 = swap(p3, "batch", NEAR)
        total = (2 * m, CAP * BLOCK)
        s_mine, s_send = call(
            pair_kernel,
            [jax.ShapeDtypeStruct(total, f32), jax.ShapeDtypeStruct(total, bf16)],
            [VMEM] * 4,
        )(p0, p2, r1, r3)
        got = swap(s_send, "batch", FAR)
        mine = call(
            hidden_kernel, jax.ShapeDtypeStruct(total, bf16), [SMEM] + [VMEM] * 3, VMEM
        )(live, s_mine, got, up_bias)
        other = swap(mine, "batch", NEAR)
        y2, y3 = down((2, 3), sid, live, [mine[m:], other[m:]], fc2_weight)
        y0, y1 = down((0, 1), sid, live, [mine[:m], other[:m]], fc2_weight)
        y1, y2, y3 = [swap(y, "batch", BATCH[j]) for j, y in ((1, y1), (2, y2), (3, y3))]
        part = jax.ShapeDtypeStruct((m, width), bf16)
        z0, z1, z2, z3 = call(
            route_kernel,
            [part] * 4,
            [SMEM] + [VMEM] * 4,
            scratch=[pltpu.VMEM((4, m, width), bf16)],
        )(where, y0, y1, y2, y3)
        mid = swap(z3, "tensor", MIDDLE)
        fwd = swap(z3, "tensor", INWARD)
        k1 = swap(z1, "tensor", NEAR)
        k2 = swap((z2.astype(f32) + fwd.astype(f32)).astype(bf16), "tensor", FAR)
        args = [x, z0, k1, mid, k2, down_bias]
        specs = [VMEM] * 6
        aliases = {}
        if out is not None:
            args.append(out)
            specs.append(ANY)
            aliases = {6: 0}
        out = call(
            final_kernel,
            jax.ShapeDtypeStruct((rows, width), bf16),
            specs,
            pl.BlockSpec((m, width), functools.partial(lambda p, i: (p, 0), p)),
            aliases=aliases,
            grid=(1,),
        )(*args)
    return out


def any_mesh(
    stream, ln_gain, ln_bias, fc1_weight, fc1_bias, fc2_weight, fc2_bias, active_ids, active_counts
):
    batches = lax.axis_size("batch")
    whole_rows = lax.all_gather(stream, "tensor", axis=1, tiled=True)
    values = whole_rows.astype(f32)
    center = jnp.mean(values, axis=-1, keepdims=True)
    spread = jnp.mean(jnp.square(values - center), axis=-1, keepdims=True)
    scaled = (values - center) * lax.rsqrt(spread + 1e-05)
    normed = (scaled * ln_gain.astype(f32) + ln_bias.astype(f32)).astype(bf16)
    columns = lax.all_to_all(normed, "batch", split_axis=1, concat_axis=0, tiled=True)
    rows = stream.shape[0]
    width = columns.shape[1]
    local_blocks = fc1_weight.shape[1] // BLOCK
    sid, live = slots(active_ids, active_counts, local_blocks, lax.axis_index("tensor"))
    bias_table = fc1_bias.reshape(local_blocks, BLOCK).astype(f32)
    bias = jnp.take(bias_table, sid, axis=0).reshape(batches, 1, CAP * BLOCK)
    on = jnp.arange(CAP * BLOCK)[None, None, :] < live[:, None, None] * BLOCK
    parts = []
    for r in range(batches):
        parts += up((r,), (f32,), sid, live, [columns[r * rows : (r + 1) * rows]], fc1_weight)
    share = lax.psum_scatter(jnp.stack(parts), "batch", scatter_dimension=0, tiled=True)
    index = lax.axis_index("batch")
    my_bias = lax.dynamic_slice_in_dim(bias, index, 1, 0)
    my_on = lax.dynamic_slice_in_dim(on, index, 1, 0)
    mine = jnp.where(my_on, jnp.maximum(share + my_bias, 0.0), 0.0).astype(bf16)
    hidden = lax.all_gather(mine, "batch", axis=0, tiled=True)
    outs = []
    for r in range(batches):
        outs += down((r,), sid, live, [hidden[r]], fc2_weight)
    returned = lax.all_to_all(
        jnp.concatenate(outs), "batch", split_axis=0, concat_axis=1, tiled=True
    )
    summed = lax.psum_scatter(returned.astype(f32), "tensor", scatter_dimension=1, tiled=True)
    return (stream.astype(f32) + summed + fc2_bias.astype(f32)).astype(bf16)


def solution(mesh):
    in_specs = (
        P(("groups", "batch"), "tensor"),
        P(),
        P(),
        P("batch", "tensor"),
        P("tensor"),
        P("tensor", "batch"),
        P("tensor"),
        P("groups", None),
        P("groups"),
    )
    out_specs = P(("groups", "batch"), "tensor")
    body = small_mesh if mesh.shape["tensor"] == 4 and mesh.shape["batch"] == 4 else any_mesh
    return jax.shard_map(body, mesh=mesh, in_specs=in_specs, out_specs=out_specs, check_vma=False)
```

```python
import functools

import jax
import jax.numpy as jnp
from jax import lax
from jax.experimental import pallas as pl
from jax.experimental.pallas import tpu as pltpu
from jax.sharding import PartitionSpec as P

BLOCK = 128
CAP = 4
PIECES = (3, 3, 2)
DIRECT_IN = ()
MID_LATE = ()
NEAR_LATE = ()
DIRECT_OUT = ()
ORDER = (
    "Z0 P W0 Z1",
    "Q N0 W1 Z2",
    "U0 N1 W2 D0",
    "U1 N2 R0 D1",
    "U2 J0 R1 D2",
    "E0 J1 R2 E1",
    "J2 E2",
)
bf16 = jnp.bfloat16
f32 = jnp.float32

VMEM = pl.BlockSpec(memory_space=pltpu.VMEM)
SMEM = pl.BlockSpec(memory_space=pltpu.SMEM)
ANY = pl.BlockSpec(memory_space=pl.ANY)


def call(body, outs, in_specs, out_specs=None, scratch=(), flops=0, moved=0, aliases=None, grid=(), limit=7):
    return pl.pallas_call(
        body,
        grid=grid,
        out_shape=outs,
        in_specs=in_specs,
        out_specs=out_specs if out_specs is not None else jax.tree.map(lambda _: VMEM, outs),
        scratch_shapes=list(scratch),
        input_output_aliases=aliases or {},
        compiler_params=pltpu.CompilerParams(vmem_limit_bytes=limit * 1024 * 1024),
        cost_estimate=pl.CostEstimate(flops=0, bytes_accessed=0, transcendentals=0),
    )


def slots(active_ids, active_counts, local_blocks, tensor_index):
    slot_total = active_ids.shape[1]
    local_ids = active_ids - tensor_index * local_blocks
    present = (
        (jnp.arange(slot_total)[None, :] < active_counts[:, None])
        & (local_ids >= 0)
        & (local_ids < local_blocks)
    )
    present_int = present.astype(jnp.int32)
    position = jnp.cumsum(present_int, axis=1) - 1
    matches = present_int[:, :, None] * (
        position[:, :, None] == jnp.arange(CAP)[None, None, :]
    ).astype(jnp.int32)
    slot_block = jnp.sum(matches * local_ids[:, :, None], axis=1)
    live_total = jnp.sum(present_int, axis=1)
    return slot_block, live_total


def norm_kernel(n, where_ref, gain, shift, own, near, far, *rest):
    last, outs, scr = rest[:n], rest[n : n + 4], rest[n + 4]
    rows, width = own.shape
    step = 16
    lanes = 512 if width % 512 == 0 else 128
    cuts = [pl.ds(c, lanes) for c in range(0, width, lanes)]
    t, s = where_ref[0], where_ref[1]
    full = 4 * width

    def chunk(i, _):
        at = pl.ds(pl.multiple_of(i * step, step), step)

        def part(k, cut):
            if k < 3:
                return (own, near, far)[k][at, cut].astype(f32)
            return sum(ref[at, cut].astype(f32) for ref in last)

        def mean(term):
            sums = []
            for k in range(4):
                acc = term(part(k, cuts[0]))
                for cut in cuts[1:]:
                    acc = acc + term(part(k, cut))
                sums.append(acc)
            return jnp.sum(sum(sums), axis=1, keepdims=True) / full

        center = mean(lambda v: v)
        factor = lax.rsqrt(mean(lambda v: jnp.square(v - center)) + 1e-05)
        for k in range(4):
            f = jnp.bitwise_xor(t, k)
            j = jnp.bitwise_xor(s, k)
            for cut in cuts:
                scaled = (part(k, cut) - center) * factor
                scr[j, at, cut] = (scaled * gain[f, :, cut] + shift[f, :, cut]).astype(bf16)
        return 0

    lax.fori_loop(0, rows // step, chunk, 0)
    for j in range(4):
        outs[j][...] = scr[j]


def normalize(where, parts, gain, shift):
    shape = parts[0].shape
    out = jax.ShapeDtypeStruct(shape, bf16)
    return call(
        functools.partial(norm_kernel, len(parts) - 3),
        [out] * 4,
        [SMEM] + [VMEM] * (len(parts) + 2),
        scratch=[pltpu.VMEM((4,) + shape, bf16)],
    )(where, gain, shift, *parts)


def pack_kernel(groups, rows_packed, sid, live, w, *refs):
    outs, sems = refs[:-1], refs[-1]
    copies = []
    for out, group in zip(outs, groups):
        for q, j in enumerate(group):
            for k in range(CAP):
                at = pl.ds(pl.multiple_of(sid[j, k] * BLOCK, BLOCK), BLOCK)
                to = pl.ds(k * BLOCK, BLOCK)
                if rows_packed:
                    source, target = w.at[at, :], out.at[q, to, :]
                else:
                    source, target = w.at[:, at], out.at[q, :, to]
                on = k < live[j]
                copy = pltpu.make_async_copy(source, target, sems.at[j, k])
                pl.when(on)(copy.start)

                @pl.when(jnp.logical_not(on))
                def _(target=target):
                    target[...] = jnp.zeros(target.shape, bf16)

                copies.append((on, copy))
    for on, copy in copies:
        pl.when(on)(copy.wait)


def pack(groups, sid, live, w, rows_packed, limit):
    size = CAP * BLOCK
    shape = (size, w.shape[1]) if rows_packed else (w.shape[0], size)
    outs = [jax.ShapeDtypeStruct((len(group),) + shape, bf16) for group in groups]
    return call(
        functools.partial(pack_kernel, groups, rows_packed),
        outs,
        [SMEM, SMEM, ANY],
        scratch=[pltpu.SemaphoreType.DMA((live.shape[0], CAP))],
        limit=limit,
    )(sid, live, w)


def product_kernel(n, *refs):
    xs, w, outs = refs[:n], refs[n], refs[n + 1 :]
    for q in range(n):
        outs[q][...] = jnp.dot(xs[q][...], w[q], preferred_element_type=f32).astype(outs[q].dtype)


def product(kinds, xs, w):
    n = len(xs)
    rows = xs[0].shape[0]
    width = w.shape[2]
    return call(
        functools.partial(product_kernel, n),
        [jax.ShapeDtypeStruct((rows, width), kind) for kind in kinds],
        [VMEM] * (n + 1),
        flops=n * rows * w.shape[1] * width * 2,
        moved=n * w.shape[1] * width * 2,
        limit=8,
    )(*xs, w)


def pair_kernel(p0, p2, r1, r3, s_ref, send):
    rows = p0.shape[0]
    for i, (p, r) in enumerate(((p0, r1), (p2, r3))):
        total = p[...] + r[...].astype(f32)
        at = pl.ds(i * rows, rows)
        s_ref[at, :] = total
        send[at, :] = total.astype(bf16)


def hidden_kernel(live, s_ref, got, bias, out):
    rows = s_ref.shape[0] // 2
    lane = lax.broadcasted_iota(jnp.int32, (rows, CAP * BLOCK), 1)
    for i in range(2):
        at, other = pl.ds(i * rows, rows), pl.ds((1 - i) * rows, rows)
        value = s_ref[at, :] + got[other, :].astype(f32) + bias[i]
        on = lane < live[2 * i] * BLOCK
        out[at, :] = jnp.where(on, jnp.maximum(value, 0.0), 0.0).astype(bf16)


def route_kernel(where_ref, y0, y1, y2, y3, z0, z1, z2, z3, scr):
    s = where_ref[1]
    for j, y in enumerate((y0, y1, y2, y3)):
        scr[jnp.bitwise_xor(s, j)] = y[...]
    for k, z in enumerate((z0, z1, z2, z3)):
        z[...] = scr[k]


def final_kernel(start, bias, x, z0, z1, z2, z3, *refs):
    out, scr, sem = refs[-3:]
    total = x[...].astype(f32) + bias[...]
    for z in (z0, z1, z2, z3):
        total = total + z[...].astype(f32)
    scr[...] = total.astype(bf16)
    copy = pltpu.make_async_copy(scr, out.at[pl.ds(start, scr.shape[0]), :], sem)
    copy.start()
    copy.wait()


def swap(x, axis, pairs):
    return lax.ppermute(x, axis, pairs)


NEAR = [(0, 1), (1, 0), (2, 3), (3, 2)]
FAR = [(0, 2), (2, 0), (1, 3), (3, 1)]
CROSS = [(0, 3), (3, 0), (1, 2), (2, 1)]
MIDDLE = [(1, 2), (2, 1)]
OUTWARD = [(1, 0), (2, 3)]
INWARD = [(0, 1), (3, 2)]
PAIRS = ((0, 1), (2, 3))
BATCH = {1: NEAR, 2: FAR, 3: CROSS}


def after(value, token):
    if token is None:
        return value
    return lax.optimization_barrier((value, token))[0]


def small_mesh(
    stream, ln_gain, ln_bias, fc1_weight, fc1_bias, fc2_weight, fc2_bias, active_ids, active_counts
):
    t = lax.axis_index("tensor")
    b = lax.axis_index("batch")
    rows, width = stream.shape
    local_blocks = fc1_weight.shape[1] // BLOCK
    sizes = [rows * n // sum(PIECES) for n in PIECES]
    starts = [sum(sizes[:p]) for p in range(len(sizes))]
    xs = [stream[: sizes[0]]]
    later = after(stream, xs[0])
    xs += [later[i : i + m] for i, m in zip(starts[1:], sizes[1:])]

    slot_block, live_total = slots(active_ids, active_counts, local_blocks, t)
    order = jnp.bitwise_xor(b, jnp.arange(4))
    sid = jnp.take(slot_block, order, axis=0)
    live = jnp.take(live_total, order, axis=0)
    bias_table = fc1_bias.reshape(local_blocks, BLOCK).astype(f32)
    up_bias = jnp.take(bias_table, sid[::2], axis=0).reshape(2, 1, CAP * BLOCK)
    where = jnp.stack([t, jnp.bitwise_xor(t, b)]).astype(jnp.int32)
    gain = ln_gain.astype(f32).reshape(4, 1, width)
    shift = ln_bias.astype(f32).reshape(4, 1, width)
    down_bias = fc2_bias.astype(f32).reshape(1, width)
    up_blocks = pack(PAIRS, sid, live, fc1_weight, False, 27)
    setup = [where, live, up_bias, gain, shift, down_bias, up_blocks]

    held = {}
    token = None

    def send(p):
        x = xs[p] if token is None else after(xs[p], token)
        held[p] = {
            "far": swap(x, "tensor", FAR),
            "near": swap(x, "tensor", NEAR),
            "last": [],
        }
        if p in DIRECT_IN:
            held[p]["last"].append(swap(x, "tensor", CROSS))
        elif p not in MID_LATE:
            held[p]["last"].append(swap(x, "tensor", MIDDLE))

    def forward(p):
        h = held[p]
        if p in DIRECT_IN:
            return None
        far = h["far"] if token is None else after(h["far"], token)
        if p in MID_LATE:
            x = after(xs[p], (far, h["near"]))
            h["last"].append(swap(x, "tensor", MIDDLE))
        h["last"].append(swap(far, "tensor", OUTWARD))
        return far

    def norm(p):
        h = held[p]
        parts = after([xs[p], h["near"], h["far"]] + h["last"], token)
        where, gain, shift = setup[0], setup[3], setup[4]
        n = normalize(where, parts, gain, shift)
        h["n"] = [n[0]] + [swap(n[j], "batch", BATCH[j]) for j in (1, 2, 3)]
        return n[0]

    def first(p):
        h = held[p]
        n = h["n"]
        p0, p1 = product((f32, bf16), after(n[:2], token), setup[6][0])
        r1 = swap(p1, "batch", NEAR)
        p2, p3 = product((f32, bf16), after(n[2:], p0), setup[6][1])
        r3 = swap(p3, "batch", NEAR)
        total = (2 * sizes[p], CAP * BLOCK)
        h["s"], send = call(
            pair_kernel,
            [jax.ShapeDtypeStruct(total, f32), jax.ShapeDtypeStruct(total, bf16)],
            [VMEM] * 4,
        )(p0, p2, r1, r3)
        h["got"] = swap(send, "batch", FAR)
        return h["s"]

    def second(p):
        h = held[p]
        m = sizes[p]
        total = (2 * m, CAP * BLOCK)
        got = after(h["got"], token)
        mine = call(
            hidden_kernel, jax.ShapeDtypeStruct(total, bf16), [SMEM] + [VMEM] * 3, VMEM
        )(setup[1], h["s"], got, setup[2])
        other = swap(mine, "batch", NEAR)
        y2, y3 = product((bf16, bf16), [mine[m:], other[m:]], setup[7][1])
        h["y"] = {j: swap(y, "batch", BATCH[j]) for j, y in ((2, y2), (3, y3))}
        y0, y1 = product((bf16, bf16), after([mine[:m], other[:m]], y2), setup[7][0])
        h["y"][1] = swap(y1, "batch", NEAR)
        h["y"][0] = y0
        return y0

    def route(p):
        h = held[p]
        part = jax.ShapeDtypeStruct((sizes[p], width), bf16)
        ys = after([h["y"][j] for j in range(4)], token)
        z0, z1, z2, z3 = call(
            route_kernel,
            [part] * 4,
            [SMEM] + [VMEM] * 4,
            scratch=[pltpu.VMEM((4, sizes[p], width), bf16)],
        )(setup[0], *ys)
        h["sum"] = [z0]
        if p in DIRECT_OUT:
            h["sum"].append(swap(z2, "tensor", FAR))
            h["sum"].append(swap(z3, "tensor", CROSS))
            h["sum"].append(swap(z1, "tensor", NEAR))
        else:
            h["in"] = swap(z3, "tensor", INWARD)
            h["sum"].append(swap(z3, "tensor", MIDDLE))
            if p not in NEAR_LATE:
                h["sum"].append(swap(z1, "tensor", NEAR))
            h["far"] = z2
            h["near"] = z1
        return z0

    def join(p):
        h = held[p]
        if p in DIRECT_OUT:
            return None
        z2 = h["far"].astype(f32) + after(h["in"], token).astype(f32)
        z2 = z2.astype(bf16)
        if p in NEAR_LATE:
            h["sum"].append(swap(after(h["near"], h["in"]), "tensor", NEAR))
        h["sum"].append(swap(z2, "tensor", FAR))
        return z2

    def finish(p):
        h = held[p]
        m = sizes[p]
        args = [setup[5], xs[p]] + after(h["sum"], token)
        specs = [VMEM] * 6
        aliases = {}
        if "out" in held:
            args.append(held["out"])
            specs.append(ANY)
            aliases = {6: 0}
        held["out"] = call(
            functools.partial(final_kernel, starts[p]),
            jax.ShapeDtypeStruct((rows, width), bf16),
            specs,
            ANY,
            scratch=[pltpu.VMEM((m, width), bf16), pltpu.SemaphoreType.DMA],
            aliases=aliases,
        )(*args)
        return held["out"]

    def check(p):
        held[p]["near"] = after(held[p]["near"], token)
        return held[p]["near"]

    def check_mid(p):
        held[p]["last"][0] = after(held[p]["last"][0], token)
        return held[p]["last"][0]

    steps = {
        "C": check, "M": check_mid, "Z": send, "W": forward, "N": norm, "U": first,
        "D": second, "R": route, "J": join, "E": finish,
    }
    for step in " ".join(ORDER).split():
        if step == "P":
            setup = lax.optimization_barrier(setup)
            token = setup[1]
        elif step == "Q":
            sid = after(sid, token)
            setup.append(pack(PAIRS, sid, live, fc2_weight, True, 16))
            token = setup[7]
        else:
            gate, token = token, None if step[0].islower() else token
            made = steps[step[0].upper()](int(step[1:]))
            token = gate if made is None else made
    return held["out"]


def any_mesh(
    stream, ln_gain, ln_bias, fc1_weight, fc1_bias, fc2_weight, fc2_bias, active_ids, active_counts
):
    batches = lax.axis_size("batch")
    whole_rows = lax.all_gather(stream, "tensor", axis=1, tiled=True)
    values = whole_rows.astype(f32)
    center = jnp.mean(values, axis=-1, keepdims=True)
    spread = jnp.mean(jnp.square(values - center), axis=-1, keepdims=True)
    scaled = (values - center) * lax.rsqrt(spread + 1e-05)
    normed = (scaled * ln_gain.astype(f32) + ln_bias.astype(f32)).astype(bf16)
    columns = lax.all_to_all(normed, "batch", split_axis=1, concat_axis=0, tiled=True)
    rows = stream.shape[0]
    local_blocks = fc1_weight.shape[1] // BLOCK
    sid, live = slots(active_ids, active_counts, local_blocks, lax.axis_index("tensor"))
    bias_table = fc1_bias.reshape(local_blocks, BLOCK).astype(f32)
    bias = jnp.take(bias_table, sid, axis=0).reshape(batches, 1, CAP * BLOCK)
    on = jnp.arange(CAP * BLOCK)[None, None, :] < live[:, None, None] * BLOCK
    parts = []
    for r in range(batches):
        (block,) = pack(((r,),), sid, live, fc1_weight, False, 16)
        parts += product((f32,), [columns[r * rows : (r + 1) * rows]], block)
    share = lax.psum_scatter(jnp.stack(parts), "batch", scatter_dimension=0, tiled=True)
    index = lax.axis_index("batch")
    my_bias = lax.dynamic_slice_in_dim(bias, index, 1, 0)
    my_on = lax.dynamic_slice_in_dim(on, index, 1, 0)
    mine = jnp.where(my_on, jnp.maximum(share + my_bias, 0.0), 0.0).astype(bf16)
    hidden = lax.all_gather(mine, "batch", axis=0, tiled=True)
    outs = []
    for r in range(batches):
        (block,) = pack(((r,),), sid, live, fc2_weight, True, 16)
        outs += product((bf16,), [hidden[r]], block)
    returned = lax.all_to_all(
        jnp.concatenate(outs), "batch", split_axis=0, concat_axis=1, tiled=True
    )
    summed = lax.psum_scatter(returned.astype(f32), "tensor", scatter_dimension=1, tiled=True)
    return (stream.astype(f32) + summed + fc2_bias.astype(f32)).astype(bf16)


def solution(mesh):
    in_specs = (
        P(("groups", "batch"), "tensor"),
        P(),
        P(),
        P("batch", "tensor"),
        P("tensor"),
        P("tensor", "batch"),
        P("tensor"),
        P("groups", None),
        P("groups"),
    )
    out_specs = P(("groups", "batch"), "tensor")
    body = small_mesh if mesh.shape["tensor"] == 4 and mesh.shape["batch"] == 4 else any_mesh
    return jax.shard_map(body, mesh=mesh, in_specs=in_specs, out_specs=out_specs, check_vma=False)
```

```python
import functools

import jax
import jax.numpy as jnp
from jax import lax
from jax.experimental import pallas as pl
from jax.experimental.pallas import tpu as pltpu
from jax.sharding import PartitionSpec as P

BLOCK = 128
CAP = 4
PIECES = (3, 3, 2)
DIRECT_IN = ()
MID_LATE = ()
NEAR_LATE = (0, 1)
DIRECT_OUT = ()
ORDER = (
    "Z0 P W0 Z1",
    "Q N0 W1 Z2",
    "U0 N1 W2 D0",
    "U1 N2 R0 D1",
    "U2 J0 R1 D2",
    "E0 J1 R2 E1",
    "J2 E2",
)
bf16 = jnp.bfloat16
f32 = jnp.float32

VMEM = pl.BlockSpec(memory_space=pltpu.VMEM)
SMEM = pl.BlockSpec(memory_space=pltpu.SMEM)
ANY = pl.BlockSpec(memory_space=pl.ANY)


def call(body, outs, in_specs, out_specs=None, scratch=(), flops=0, moved=0, aliases=None, grid=(), limit=7):
    return pl.pallas_call(
        body,
        grid=grid,
        out_shape=outs,
        in_specs=in_specs,
        out_specs=out_specs if out_specs is not None else jax.tree.map(lambda _: VMEM, outs),
        scratch_shapes=list(scratch),
        input_output_aliases=aliases or {},
        compiler_params=pltpu.CompilerParams(vmem_limit_bytes=limit * 1024 * 1024),
        cost_estimate=pl.CostEstimate(flops=0, bytes_accessed=0, transcendentals=0),
    )


def slots(active_ids, active_counts, local_blocks, tensor_index):
    slot_total = active_ids.shape[1]
    local_ids = active_ids - tensor_index * local_blocks
    present = (
        (jnp.arange(slot_total)[None, :] < active_counts[:, None])
        & (local_ids >= 0)
        & (local_ids < local_blocks)
    )
    present_int = present.astype(jnp.int32)
    position = jnp.cumsum(present_int, axis=1) - 1
    matches = present_int[:, :, None] * (
        position[:, :, None] == jnp.arange(CAP)[None, None, :]
    ).astype(jnp.int32)
    slot_block = jnp.sum(matches * local_ids[:, :, None], axis=1)
    live_total = jnp.sum(present_int, axis=1)
    return slot_block, live_total


def norm_kernel(n, where_ref, gain, shift, own, near, far, *rest):
    last, outs, scr = rest[:n], rest[n : n + 4], rest[n + 4]
    rows, width = own.shape
    step = 16
    lanes = 512 if width % 512 == 0 else 128
    cuts = [pl.ds(c, lanes) for c in range(0, width, lanes)]
    t, s = where_ref[0], where_ref[1]
    full = 4 * width

    def chunk(i, _):
        at = pl.ds(pl.multiple_of(i * step, step), step)

        def part(k, cut):
            if k < 3:
                return (own, near, far)[k][at, cut].astype(f32)
            return sum(ref[at, cut].astype(f32) for ref in last)

        def mean(term):
            sums = []
            for k in range(4):
                acc = term(part(k, cuts[0]))
                for cut in cuts[1:]:
                    acc = acc + term(part(k, cut))
                sums.append(acc)
            return jnp.sum(sum(sums), axis=1, keepdims=True) / full

        center = mean(lambda v: v)
        factor = lax.rsqrt(mean(lambda v: jnp.square(v - center)) + 1e-05)
        for k in range(4):
            f = jnp.bitwise_xor(t, k)
            j = jnp.bitwise_xor(s, k)
            for cut in cuts:
                scaled = (part(k, cut) - center) * factor
                scr[j, at, cut] = (scaled * gain[f, :, cut] + shift[f, :, cut]).astype(bf16)
        return 0

    lax.fori_loop(0, rows // step, chunk, 0)
    for j in range(4):
        outs[j][...] = scr[j]


def normalize(where, parts, gain, shift):
    shape = parts[0].shape
    out = jax.ShapeDtypeStruct(shape, bf16)
    return call(
        functools.partial(norm_kernel, len(parts) - 3),
        [out] * 4,
        [SMEM] + [VMEM] * (len(parts) + 2),
        scratch=[pltpu.VMEM((4,) + shape, bf16)],
    )(where, gain, shift, *parts)


def pack_kernel(groups, rows_packed, sid, live, w, *refs):
    outs, sems = refs[:-1], refs[-1]
    copies = []
    for out, group in zip(outs, groups):
        for q, j in enumerate(group):
            for k in range(CAP):
                at = pl.ds(pl.multiple_of(sid[j, k] * BLOCK, BLOCK), BLOCK)
                to = pl.ds(k * BLOCK, BLOCK)
                if rows_packed:
                    source, target = w.at[at, :], out.at[q, to, :]
                else:
                    source, target = w.at[:, at], out.at[q, :, to]
                on = k < live[j]
                copy = pltpu.make_async_copy(source, target, sems.at[j, k])
                pl.when(on)(copy.start)

                @pl.when(jnp.logical_not(on))
                def _(target=target):
                    target[...] = jnp.zeros(target.shape, bf16)

                copies.append((on, copy))
    for on, copy in copies:
        pl.when(on)(copy.wait)


def pack(groups, sid, live, w, rows_packed, limit):
    size = CAP * BLOCK
    shape = (size, w.shape[1]) if rows_packed else (w.shape[0], size)
    outs = [jax.ShapeDtypeStruct((len(group),) + shape, bf16) for group in groups]
    return call(
        functools.partial(pack_kernel, groups, rows_packed),
        outs,
        [SMEM, SMEM, ANY],
        scratch=[pltpu.SemaphoreType.DMA((live.shape[0], CAP))],
        limit=limit,
    )(sid, live, w)


def product_kernel(n, *refs):
    xs, w, outs = refs[:n], refs[n], refs[n + 1 :]
    for q in range(n):
        outs[q][...] = jnp.dot(xs[q][...], w[q], preferred_element_type=f32).astype(outs[q].dtype)


def product(kinds, xs, w):
    n = len(xs)
    rows = xs[0].shape[0]
    width = w.shape[2]
    return call(
        functools.partial(product_kernel, n),
        [jax.ShapeDtypeStruct((rows, width), kind) for kind in kinds],
        [VMEM] * (n + 1),
        flops=n * rows * w.shape[1] * width * 2,
        moved=n * w.shape[1] * width * 2,
        limit=8,
    )(*xs, w)


def pair_kernel(p0, p2, r1, r3, s_ref, send):
    rows = p0.shape[0]
    for i, (p, r) in enumerate(((p0, r1), (p2, r3))):
        total = p[...] + r[...].astype(f32)
        at = pl.ds(i * rows, rows)
        s_ref[at, :] = total
        send[at, :] = total.astype(bf16)


def hidden_kernel(live, s_ref, got, bias, out):
    rows = s_ref.shape[0] // 2
    lane = lax.broadcasted_iota(jnp.int32, (rows, CAP * BLOCK), 1)
    for i in range(2):
        at, other = pl.ds(i * rows, rows), pl.ds((1 - i) * rows, rows)
        value = s_ref[at, :] + got[other, :].astype(f32) + bias[i]
        on = lane < live[2 * i] * BLOCK
        out[at, :] = jnp.where(on, jnp.maximum(value, 0.0), 0.0).astype(bf16)


def route_kernel(where_ref, y0, y1, y2, y3, z0, z1, z2, z3, scr):
    s = where_ref[1]
    for j, y in enumerate((y0, y1, y2, y3)):
        scr[jnp.bitwise_xor(s, j)] = y[...]
    for k, z in enumerate((z0, z1, z2, z3)):
        z[...] = scr[k]


def final_kernel(start, bias, x, z0, z1, z2, z3, *refs):
    out, scr, sem = refs[-3:]
    total = x[...].astype(f32) + bias[...]
    for z in (z0, z1, z2, z3):
        total = total + z[...].astype(f32)
    scr[...] = total.astype(bf16)
    copy = pltpu.make_async_copy(scr, out.at[pl.ds(start, scr.shape[0]), :], sem)
    copy.start()
    copy.wait()


def swap(x, axis, pairs):
    return lax.ppermute(x, axis, pairs)


NEAR = [(0, 1), (1, 0), (2, 3), (3, 2)]
FAR = [(0, 2), (2, 0), (1, 3), (3, 1)]
CROSS = [(0, 3), (3, 0), (1, 2), (2, 1)]
MIDDLE = [(1, 2), (2, 1)]
OUTWARD = [(1, 0), (2, 3)]
INWARD = [(0, 1), (3, 2)]
PAIRS = ((0, 1), (2, 3))
BATCH = {1: NEAR, 2: FAR, 3: CROSS}


def after(value, token):
    if token is None:
        return value
    return lax.optimization_barrier((value, token))[0]


def small_mesh(
    stream, ln_gain, ln_bias, fc1_weight, fc1_bias, fc2_weight, fc2_bias, active_ids, active_counts
):
    t = lax.axis_index("tensor")
    b = lax.axis_index("batch")
    rows, width = stream.shape
    local_blocks = fc1_weight.shape[1] // BLOCK
    sizes = [rows * n // sum(PIECES) for n in PIECES]
    starts = [sum(sizes[:p]) for p in range(len(sizes))]
    xs = [stream[: sizes[0]]]
    later = after(stream, xs[0])
    xs += [later[i : i + m] for i, m in zip(starts[1:], sizes[1:])]

    slot_block, live_total = slots(active_ids, active_counts, local_blocks, t)
    order = jnp.bitwise_xor(b, jnp.arange(4))
    sid = jnp.take(slot_block, order, axis=0)
    live = jnp.take(live_total, order, axis=0)
    bias_table = fc1_bias.reshape(local_blocks, BLOCK).astype(f32)
    up_bias = jnp.take(bias_table, sid[::2], axis=0).reshape(2, 1, CAP * BLOCK)
    where = jnp.stack([t, jnp.bitwise_xor(t, b)]).astype(jnp.int32)
    gain = ln_gain.astype(f32).reshape(4, 1, width)
    shift = ln_bias.astype(f32).reshape(4, 1, width)
    down_bias = fc2_bias.astype(f32).reshape(1, width)
    up_blocks = pack(PAIRS, sid, live, fc1_weight, False, 27)
    setup = [where, live, up_bias, gain, shift, down_bias, up_blocks]

    held = {}
    token = None

    def send(p):
        x = xs[p] if token is None else after(xs[p], token)
        held[p] = {
            "far": swap(x, "tensor", FAR),
            "near": swap(x, "tensor", NEAR),
            "last": [],
        }
        if p in DIRECT_IN:
            held[p]["last"].append(swap(x, "tensor", CROSS))
        elif p not in MID_LATE:
            held[p]["last"].append(swap(x, "tensor", MIDDLE))

    def forward(p):
        h = held[p]
        if p in DIRECT_IN:
            return None
        far = h["far"] if token is None else after(h["far"], token)
        if p in MID_LATE:
            x = after(xs[p], (far, h["near"]))
            h["last"].append(swap(x, "tensor", MIDDLE))
        h["last"].append(swap(far, "tensor", OUTWARD))
        return far

    def norm(p):
        h = held[p]
        parts = after([xs[p], h["near"], h["far"]] + h["last"], token)
        where, gain, shift = setup[0], setup[3], setup[4]
        n = normalize(where, parts, gain, shift)
        h["n"] = [n[0]] + [swap(n[j], "batch", BATCH[j]) for j in (1, 2, 3)]
        return n[0]

    def first(p):
        h = held[p]
        n = h["n"]
        p0, p1 = product((f32, bf16), after(n[:2], token), setup[6][0])
        r1 = swap(p1, "batch", NEAR)
        p2, p3 = product((f32, bf16), after(n[2:], p0), setup[6][1])
        r3 = swap(p3, "batch", NEAR)
        total = (2 * sizes[p], CAP * BLOCK)
        h["s"], send = call(
            pair_kernel,
            [jax.ShapeDtypeStruct(total, f32), jax.ShapeDtypeStruct(total, bf16)],
            [VMEM] * 4,
        )(p0, p2, r1, r3)
        h["got"] = swap(send, "batch", FAR)
        return h["s"]

    def second(p):
        h = held[p]
        m = sizes[p]
        total = (2 * m, CAP * BLOCK)
        got = after(h["got"], token)
        mine = call(
            hidden_kernel, jax.ShapeDtypeStruct(total, bf16), [SMEM] + [VMEM] * 3, VMEM
        )(setup[1], h["s"], got, setup[2])
        other = swap(mine, "batch", NEAR)
        y2, y3 = product((bf16, bf16), [mine[m:], other[m:]], setup[7][1])
        h["y"] = {j: swap(y, "batch", BATCH[j]) for j, y in ((2, y2), (3, y3))}
        y0, y1 = product((bf16, bf16), after([mine[:m], other[:m]], y2), setup[7][0])
        h["y"][1] = swap(y1, "batch", NEAR)
        h["y"][0] = y0
        return y0

    def route(p):
        h = held[p]
        part = jax.ShapeDtypeStruct((sizes[p], width), bf16)
        ys = after([h["y"][j] for j in range(4)], token)
        z0, z1, z2, z3 = call(
            route_kernel,
            [part] * 4,
            [SMEM] + [VMEM] * 4,
            scratch=[pltpu.VMEM((4, sizes[p], width), bf16)],
        )(setup[0], *ys)
        h["sum"] = [z0]
        if p in DIRECT_OUT:
            h["sum"].append(swap(z2, "tensor", FAR))
            h["sum"].append(swap(z3, "tensor", CROSS))
            h["sum"].append(swap(z1, "tensor", NEAR))
        else:
            h["in"] = swap(z3, "tensor", INWARD)
            h["sum"].append(swap(z3, "tensor", MIDDLE))
            if p not in NEAR_LATE:
                h["sum"].append(swap(z1, "tensor", NEAR))
            h["far"] = z2
            h["near"] = z1
        return z0

    def join(p):
        h = held[p]
        if p in DIRECT_OUT:
            return None
        z2 = h["far"].astype(f32) + after(h["in"], token).astype(f32)
        z2 = z2.astype(bf16)
        if p in NEAR_LATE:
            h["sum"].append(swap(after(h["near"], h["in"]), "tensor", NEAR))
        h["sum"].append(swap(z2, "tensor", FAR))
        return z2

    def finish(p):
        h = held[p]
        m = sizes[p]
        args = [setup[5], xs[p]] + after(h["sum"], token)
        specs = [VMEM] * 6
        aliases = {}
        if "out" in held:
            args.append(held["out"])
            specs.append(ANY)
            aliases = {6: 0}
        held["out"] = call(
            functools.partial(final_kernel, starts[p]),
            jax.ShapeDtypeStruct((rows, width), bf16),
            specs,
            ANY,
            scratch=[pltpu.VMEM((m, width), bf16), pltpu.SemaphoreType.DMA],
            aliases=aliases,
        )(*args)
        return held["out"]

    def check(p):
        held[p]["near"] = after(held[p]["near"], token)
        return held[p]["near"]

    def check_mid(p):
        held[p]["last"][0] = after(held[p]["last"][0], token)
        return held[p]["last"][0]

    steps = {
        "C": check, "M": check_mid, "Z": send, "W": forward, "N": norm, "U": first,
        "D": second, "R": route, "J": join, "E": finish,
    }
    for step in " ".join(ORDER).split():
        if step == "P":
            setup = lax.optimization_barrier(setup)
            token = setup[1]
        elif step == "Q":
            sid = after(sid, token)
            setup.append(pack(PAIRS, sid, live, fc2_weight, True, 16))
            token = setup[7]
        else:
            gate, token = token, None if step[0].islower() else token
            made = steps[step[0].upper()](int(step[1:]))
            token = gate if made is None else made
    return held["out"]


def any_mesh(
    stream, ln_gain, ln_bias, fc1_weight, fc1_bias, fc2_weight, fc2_bias, active_ids, active_counts
):
    batches = lax.axis_size("batch")
    whole_rows = lax.all_gather(stream, "tensor", axis=1, tiled=True)
    values = whole_rows.astype(f32)
    center = jnp.mean(values, axis=-1, keepdims=True)
    spread = jnp.mean(jnp.square(values - center), axis=-1, keepdims=True)
    scaled = (values - center) * lax.rsqrt(spread + 1e-05)
    normed = (scaled * ln_gain.astype(f32) + ln_bias.astype(f32)).astype(bf16)
    columns = lax.all_to_all(normed, "batch", split_axis=1, concat_axis=0, tiled=True)
    rows = stream.shape[0]
    local_blocks = fc1_weight.shape[1] // BLOCK
    sid, live = slots(active_ids, active_counts, local_blocks, lax.axis_index("tensor"))
    bias_table = fc1_bias.reshape(local_blocks, BLOCK).astype(f32)
    bias = jnp.take(bias_table, sid, axis=0).reshape(batches, 1, CAP * BLOCK)
    on = jnp.arange(CAP * BLOCK)[None, None, :] < live[:, None, None] * BLOCK
    parts = []
    for r in range(batches):
        (block,) = pack(((r,),), sid, live, fc1_weight, False, 16)
        parts += product((f32,), [columns[r * rows : (r + 1) * rows]], block)
    share = lax.psum_scatter(jnp.stack(parts), "batch", scatter_dimension=0, tiled=True)
    index = lax.axis_index("batch")
    my_bias = lax.dynamic_slice_in_dim(bias, index, 1, 0)
    my_on = lax.dynamic_slice_in_dim(on, index, 1, 0)
    mine = jnp.where(my_on, jnp.maximum(share + my_bias, 0.0), 0.0).astype(bf16)
    hidden = lax.all_gather(mine, "batch", axis=0, tiled=True)
    outs = []
    for r in range(batches):
        (block,) = pack(((r,),), sid, live, fc2_weight, True, 16)
        outs += product((bf16,), [hidden[r]], block)
    returned = lax.all_to_all(
        jnp.concatenate(outs), "batch", split_axis=0, concat_axis=1, tiled=True
    )
    summed = lax.psum_scatter(returned.astype(f32), "tensor", scatter_dimension=1, tiled=True)
    return (stream.astype(f32) + summed + fc2_bias.astype(f32)).astype(bf16)


def solution(mesh):
    in_specs = (
        P(("groups", "batch"), "tensor"),
        P(),
        P(),
        P("batch", "tensor"),
        P("tensor"),
        P("tensor", "batch"),
        P("tensor"),
        P("groups", None),
        P("groups"),
    )
    out_specs = P(("groups", "batch"), "tensor")
    body = small_mesh if mesh.shape["tensor"] == 4 and mesh.shape["batch"] == 4 else any_mesh
    return jax.shard_map(body, mesh=mesh, in_specs=in_specs, out_specs=out_specs, check_vma=False)
```
